32 devices in a mesh: groups: 2 (over y), row: 8 (over z, x), col: 2 (over core).
Axes of the slice: x: 2, y: 2, z: 4, core: 2. Of those that a mesh axis runs over, the one named last changes fastest.
Arguments:
- points: bfloat16 [64, 6144], P(None, ('groups', 'row', 'col')), parts along dimension 1, may hold values from -8.5 to 8.5
- direction: float32 [32, 6144], P(None, ('groups', 'row', 'col')), parts along dimension 1, may hold values from -80 to 80
- residual: float32 [32, 6144], P(None, ('groups', 'row', 'col')), parts along dimension 1, may hold values from -80 to 80
- solution: float32 [32, 6144], P(None, ('groups', 'row', 'col')), parts along dimension 1, may hold values from -6 to 6
Outputs:
- solution_next: float32 [32, 6144], P(None, ('groups', 'row', 'col')), parts along dimension 1
- residual_next: float32 [32, 6144], P(None, ('groups', 'row', 'col')), parts along dimension 1
- direction_next: float32 [32, 6144], P(None, ('groups', 'row', 'col')), parts along dimension 1
The draws below stay inside these ranges and needn't reach their ends.
There are 2 independent parts, one for each index of `groups`. The reference program is written for one: setup_inputs(seed, part) draws one part's arguments, and reference() takes and returns one part's arrays. A program takes and returns all parts, laid end to end along the dimension named above; each array names one. Nothing has to cross between parts.
All inputs are finite; a program needn't handle non-finite values.
Results may differ from the reference program's by a relative error of at most 0.0027.
Values may be sent and summed in bfloat16 or wider, within the bound.
No kernel may reach another device: no remote copies, remote signals or barrier semaphores. Data moves between devices by JAX's collectives and lax.ppermute only.
A program may use at most 64 MiB of HBM per device.

```python
import math
import jax
import jax.numpy as jnp
from jax import lax

DIM = 64
PROBES = 32
POINTS = 3072


def spread(key, base):
    first_key, second_key = jax.random.split(key)
    position = jnp.arange(POINTS, dtype=jnp.float32) / POINTS
    row_scale = jnp.exp(jnp.log(3.0) * position + jnp.log(4.0) * jax.random.uniform(first_key, (POINTS,)))
    col_scale = jnp.exp(jnp.log(10.0) * jax.random.uniform(second_key, (PROBES, 1)))
    return base * row_scale[None, :] * col_scale / 8.0


def draw_points(key, part):
    key = jax.random.fold_in(key, 7)
    values = jnp.clip(1.4142 * jax.random.normal(key, (DIM, POINTS)), -8.5, 8.5)
    return values.astype(jnp.bfloat16)


def draw_residual(key, part):
    key = jax.random.fold_in(key, 11)
    first_key, second_key = jax.random.split(key)
    base = jnp.clip(jax.random.normal(first_key, (PROBES, POINTS)), -5.0, 5.0)
    return spread(second_key, base)


def draw_direction(key, part):
    key = jax.random.fold_in(key, 13)
    first_key, second_key = jax.random.split(key)
    base = jnp.clip(jax.random.normal(first_key, (PROBES, POINTS)), -5.0, 5.0)
    return spread(second_key, base)


def steps_of(own_key, dims, shards, low, high):
    loudness, own = 1.0, jax.random.fold_in(own_key, 6)
    for dim, shards_of in shards:
        draws = jnp.exp(jax.random.uniform(jax.random.fold_in(own, dim), (shards_of,), jnp.float32, low / len(shards), high / len(shards)))
        loudness = loudness * jnp.repeat(draws, dims[dim] // shards_of).reshape([-1 if axis == dim else 1 for axis in range(len(dims))])
    return loudness


def noise(own_key, shape, scale, bound, cuts=(), kind=jnp.bfloat16):
    drawn = scale * jax.random.normal(own_key, shape, jnp.float32)
    if cuts:
        drawn = drawn * steps_of(own_key, shape, cuts, -0.22, 0.18)
    return jnp.clip(drawn, -bound, bound).astype(kind)


def setup_inputs(seed: int = 0, part: int = 0) -> dict:
    splits = jax.random.split(jax.random.key(seed), 5)
    part_splits = jax.random.split(jax.random.fold_in(splits[4], part), 5)
    return {
        "points": draw_points(jax.random.fold_in(jax.random.fold_in(splits[4], part), 71), part),
        "direction": draw_direction(jax.random.fold_in(jax.random.fold_in(splits[4], part), 71), part),
        "residual": draw_residual(jax.random.fold_in(jax.random.fold_in(splits[4], part), 71), part),
        "solution": noise(part_splits[3], (PROBES, POINTS), 1.0, 6.0, ((1, 16),), jnp.float32),
    }


amplitude = 1.0
length_square = 32.0
noise_level = 0.5


def squares(points):
    widened = points.astype(jnp.float32)
    return jnp.sum(widened * widened, axis=0)


def kernel_tile(row_points, row_square, col_points, col_square):
    products = lax.dot_general(row_points, col_points, (((0,), (0,)), ((), ())), preferred_element_type=jnp.float32)
    distance = row_square[:, None] + col_square[None, :] - 2.0 * products
    return (amplitude * jnp.exp(-distance / (2.0 * length_square))).astype(jnp.bfloat16)


def reference(points, direction, residual, solution):
    probes = direction.astype(jnp.bfloat16)
    square = squares(points)
    block_size = math.gcd(POINTS, 512)
    block_count = POINTS // block_size

    def one_block(offset):
        row_points = lax.dynamic_slice_in_dim(points, offset, block_size, 1)
        row_square = lax.dynamic_slice_in_dim(square, offset, block_size, 0)
        kernel = kernel_tile(row_points, row_square, points, square)
        return lax.dot_general(probes, kernel, (((1,), (1,)), ((), ())), preferred_element_type=jnp.float32)

    starts = (jnp.arange(block_count) * block_size).astype(jnp.int32)
    pieces = lax.map(one_block, starts)
    applied = jnp.transpose(pieces, (1, 0, 2)).reshape(PROBES, POINTS)
    image = applied + noise_level * direction
    old_norm = jnp.sum(residual * residual, axis=1)
    curvature = jnp.sum(direction * image, axis=1)
    step_size = old_norm / curvature
    solution_next = solution + step_size[:, None] * direction
    residual_next = residual - step_size[:, None] * image
    new_norm = jnp.sum(residual_next * residual_next, axis=1)
    direction_next = residual_next + (new_norm / (old_norm + 1e-6))[:, None] * direction
    return (solution_next, residual_next, direction_next)
```

```python
import math

import jax
import jax.numpy as jnp
from jax import lax
from jax.sharding import PartitionSpec as P

amplitude = 1.0
length_square = 32.0
noise_level = 0.5

AXES = ("row", "col")


def squares(points):
    widened = points.astype(jnp.float32)
    return jnp.sum(widened * widened, axis=0)


def kernel_tile(row_points, row_square, col_points, col_square):
    products = lax.dot_general(
        row_points, col_points, (((0,), (0,)), ((), ())), preferred_element_type=jnp.float32
    )
    distance = row_square[:, None] + col_square[None, :] - 2.0 * products
    return (amplitude * jnp.exp(-distance / (2.0 * length_square))).astype(jnp.bfloat16)


def fold_columns(row_points, running_sum, pieces):
    row_square = squares(row_points)
    col_points, col_probes = pieces
    column_count = col_points.shape[1]
    block_size = math.gcd(column_count, 2048)

    def one_block(block_index, running):
        offset = block_index * block_size
        part_points = lax.dynamic_slice_in_dim(col_points, offset, block_size, 1)
        part_probes = lax.dynamic_slice_in_dim(col_probes, offset, block_size, 1)
        kernel = kernel_tile(row_points, row_square, part_points, squares(part_points))
        return running + lax.dot_general(
            part_probes, kernel, (((1,), (1,)), ((), ())), preferred_element_type=jnp.float32
        )

    return lax.fori_loop(0, column_count // block_size, one_block, running_sum)


def strides(count):
    found = []
    while count > 1:
        assert count % 2 == 0
        count //= 2
        found.append(count)
    return found


def swapped(array, count, stride):
    return lax.ppermute(array, AXES, [(i, i ^ stride) for i in range(count)])


def make_body(count):
    def total(values):
        for stride in reversed(strides(count)):
            values = values + swapped(values, count, stride)
        return values

    def body(points, direction, residual, solution):
        probes = direction.astype(jnp.bfloat16)
        held = jnp.concatenate([points, probes], axis=0)[None]
        for stride in strides(count):
            held = jnp.concatenate([held, swapped(held, count, stride)], axis=0)
        held = jnp.transpose(held, (1, 0, 2)).reshape(held.shape[1], -1)
        initial = jnp.zeros((probes.shape[0], points.shape[1]), jnp.float32)
        applied = fold_columns(points, initial, (held[: points.shape[0]], held[points.shape[0] :]))
        image = applied + noise_level * direction
        sums = total(
            jnp.stack(
                [
                    jnp.sum(residual * residual, axis=1),
                    jnp.sum(direction * image, axis=1),
                    jnp.sum(residual * image, axis=1),
                    jnp.sum(image * image, axis=1),
                ]
            )
        )
        old_norm, curvature, cross, image_norm = sums[0], sums[1], sums[2], sums[3]
        step_size = old_norm / curvature
        solution_next = solution + step_size[:, None] * direction
        residual_next = residual - step_size[:, None] * image
        new_norm = old_norm + step_size * (step_size * image_norm - 2.0 * cross)
        direction_next = residual_next + (new_norm / (old_norm + 1e-06))[:, None] * direction
        return (solution_next, residual_next, direction_next)

    return body


def solution(mesh):
    placed = P(None, ("groups", "row", "col"))
    return jax.shard_map(
        make_body(mesh.shape["row"] * mesh.shape["col"]),
        mesh=mesh,
        in_specs=(placed,) * 4,
        out_specs=(placed,) * 3,
        check_vma=False,
    )
```

```python
import functools
import math

import jax
import jax.numpy as jnp
from jax import lax
from jax.experimental import pallas as pl
from jax.experimental.pallas import tpu as pltpu
from jax.sharding import PartitionSpec as P

amplitude = 1.0
length_square = 32.0
noise_level = 0.5

AXES = ("row", "col")
LANES = 128
VMEM_BYTES = 32 << 20
RATE = math.log2(math.e) / length_square
SHIFT = math.log2(amplitude)


def in_vmem():
    return pl.BlockSpec(memory_space=pltpu.VMEM)


def halves(values):
    high = values.astype(jnp.bfloat16)
    return high, (values - high.astype(jnp.float32)).astype(jnp.bfloat16)


def pack_kernel(points_ref, direction_ref, residual_ref, out_ref):
    direction_high, direction_low = halves(direction_ref[...])
    residual_high, residual_low = halves(residual_ref[...])
    fields = jnp.concatenate(
        [points_ref[...], direction_high, residual_high, residual_low, direction_low], axis=0
    )
    height = fields.shape[0]
    out_ref[:height] = fields[:, :LANES]
    out_ref[height:] = jnp.concatenate(
        [fields[: height // 2, LANES:], fields[height // 2 :, LANES:]], axis=1
    )


def unpack_kernel(dim, first_ref, second_ref, held_ref, residual_ref, direction_ref):
    packs = [first_ref[0], first_ref[1], second_ref[0], second_ref[1]]
    side = LANES // 2
    height = packs[0].shape[0] * 2 // 3
    middle = height // 2
    probes = middle - dim
    upper, lower = [], []
    for pack in packs:
        upper.append(pack[:middle])
        lower.append(pack[middle:height])
    for left, right in ((packs[0], packs[1]), (packs[2], packs[3])):
        left, right = left[height:], right[height:]
        upper.append(jnp.concatenate([left[:, :side], right[:, :side]], axis=1))
        lower.append(jnp.concatenate([left[:, side:], right[:, side:]], axis=1))
    for index in range(len(upper)):
        span = slice(index * LANES, (index + 1) * LANES)
        held_ref[:, span] = upper[index]
        low = lower[index].astype(jnp.float32)
        residual_ref[:, span] = low[:probes] + low[probes : 2 * probes]
        direction_ref[:, span] = upper[index][dim:].astype(jnp.float32) + low[2 * probes :]


def widened(points, own):
    values = points.astype(jnp.float32)
    half = -0.5 * jnp.sum(values * values, axis=0, keepdims=True)
    high = half.astype(jnp.bfloat16).astype(jnp.float32)
    middle = (half - high).astype(jnp.bfloat16).astype(jnp.float32)
    low = half - high - middle
    row = lax.broadcasted_iota(jnp.int32, (16, points.shape[1]), 0)
    base = 0 if own else 3
    extra = jnp.where(row < 6, 1.0, 0.0)
    extra = jnp.where(row == base, high, extra)
    extra = jnp.where(row == base + 1, middle, extra)
    extra = jnp.where(row == base + 2, low, extra)
    return jnp.concatenate([points, extra.astype(jnp.bfloat16)], axis=0)


def fold(own, pieces, applied, dim):
    own_points = widened(own[:dim], True)
    for piece in pieces:
        half = lax.dot_general(
            widened(piece[:dim], False),
            own_points,
            (((0,), (0,)), ((), ())),
            preferred_element_type=jnp.float32,
        )
        kernel = jnp.exp2(half * RATE + SHIFT).astype(jnp.bfloat16)
        part = lax.dot_general(
            piece[dim:], kernel, (((1,), (0,)), ((), ())), preferred_element_type=jnp.float32
        )
        applied = part if applied is None else applied + part
    return applied


def first_fold_kernel(dim, own_ref, applied_ref):
    own = own_ref[...]
    applied_ref[...] = fold(own, [own], None, dim)


def fold_kernel(dim, own_ref, pieces_ref, before_ref, applied_ref):
    pieces = [pieces_ref[index] for index in range(pieces_ref.shape[0])]
    applied_ref[...] = fold(own_ref[...], pieces, before_ref[...], dim)


def long_fold_kernel(dim, own_ref, piece_ref, before_ref, applied_ref):
    @pl.when(pl.program_id(0) == 0)
    def _():
        applied_ref[...] = before_ref[...]

    applied_ref[...] = fold(own_ref[...], [piece_ref[0]], applied_ref[...], dim)


def sums_kernel(applied_ref, residual_ref, direction_ref, sums_ref):
    residual, direction = residual_ref[...], direction_ref[...]
    image = applied_ref[...] + noise_level * direction
    lane = lax.broadcasted_iota(jnp.int32, (image.shape[0], LANES), 1)
    table = jnp.zeros((image.shape[0], LANES), jnp.float32)
    products = (residual * residual, direction * image, residual * image, image * image)
    for index, product in enumerate(products):
        table = jnp.where(lane == index, jnp.sum(product, axis=1, keepdims=True), table)
    sums_ref[...] = table.T[:8]


def last_kernel(dim, own_ref, pieces_ref, before_ref, residual_ref, direction_ref, applied_ref, sums_ref):
    fold_kernel(dim, own_ref, pieces_ref, before_ref, applied_ref)
    sums_kernel(applied_ref, residual_ref, direction_ref, sums_ref)


def call(kernel, outs, args, pieces=0):
    columns, dim = 768, 80
    cost = None
    if pieces:
        count = pieces * columns * columns
        cost = pl.CostEstimate(
            flops=2 * count * (dim + 32), bytes_accessed=count, transcendentals=count
        )
    return pl.pallas_call(
        kernel,
        out_shape=outs,
        in_specs=[in_vmem()] * len(args),
        out_specs=jax.tree.map(lambda _: in_vmem(), outs),
        compiler_params=pltpu.CompilerParams(vmem_limit_bytes=VMEM_BYTES),
        cost_estimate=cost,
    )(*args)


def long_fold(own, pieces, before, dim):
    whole = lambda index: (0, 0)
    return pl.pallas_call(
        functools.partial(long_fold_kernel, dim),
        grid=(pieces.shape[0],),
        out_shape=jax.ShapeDtypeStruct(before.shape, before.dtype),
        in_specs=[
            pl.BlockSpec(own.shape, whole),
            pl.BlockSpec((1, *pieces.shape[1:]), lambda index: (index, 0, 0)),
            pl.BlockSpec(before.shape, whole),
        ],
        out_specs=pl.BlockSpec(before.shape, whole),
        compiler_params=pltpu.CompilerParams(vmem_limit_bytes=VMEM_BYTES),
    )(own, pieces, before)


def strides(count):
    found = []
    while count > 1:
        assert count % 2 == 0
        count //= 2
        found.append(count)
    return found


def swapped(array, count, stride):
    return lax.ppermute(array, AXES, [(i, i ^ stride) for i in range(count)])


def make_body(count):
    far, middle, *near = strides(count)

    def body(points, direction, residual, solution):
        dim, width = points.shape
        probes = direction.shape[0]
        columns = 4 * width
        height = dim + 4 * probes
        full = jax.ShapeDtypeStruct((probes, columns), jnp.float32)
        table = jax.ShapeDtypeStruct((8, probes), jnp.float32)
        packed = call(
            pack_kernel,
            jax.ShapeDtypeStruct((height * 3 // 2, LANES), jnp.bfloat16),
            (points, direction, residual),
        )[None]
        pair = jnp.concatenate([packed, swapped(packed, count, far)], axis=0)
        other = swapped(pair, count, middle)
        own, all_residual, all_direction = call(
            functools.partial(unpack_kernel, dim),
            (jax.ShapeDtypeStruct((dim + probes, columns), jnp.bfloat16), full, full),
            (pair, other),
        )
        held = own[None]
        applied = None
        pieces = None
        for stride in near:
            arriving = swapped(held, count, stride)
            if applied is None:
                applied = call(functools.partial(first_fold_kernel, dim), full, (own,), 1)
            elif pieces.shape[0] <= 2:
                applied = call(
                    functools.partial(fold_kernel, dim), full, (own, pieces, applied), pieces.shape[0]
                )
            else:
                applied = long_fold(own, pieces, applied, dim)
            held = jnp.concatenate([held, arriving], axis=0)
            pieces = arriving
        if pieces.shape[0] <= 2:
            applied, sums = call(
                functools.partial(last_kernel, dim),
                (full, table),
                (own, pieces, applied, all_residual, all_direction),
                pieces.shape[0],
            )
        else:
            applied = long_fold(own, pieces, applied, dim)
            sums = call(sums_kernel, table, (applied, all_residual, all_direction))
        for stride in reversed(near):
            sums = sums + swapped(sums, count, stride)
        start = 4 * LANES
        applied = jnp.concatenate([applied[:, :LANES], applied[:, start : start + width - LANES]], axis=1)
        image = applied + noise_level * direction
        old_norm, curvature, cross, image_norm = sums[0], sums[1], sums[2], sums[3]
        step_size = old_norm / curvature
        solution_next = solution + step_size[:, None] * direction
        residual_next = residual - step_size[:, None] * image
        new_norm = old_norm + step_size * (step_size * image_norm - 2.0 * cross)
        direction_next = residual_next + (new_norm / (old_norm + 1e-06))[:, None] * direction
        return (solution_next, residual_next, direction_next)

    return body


def solution(mesh):
    placed = P(None, ("groups", "row", "col"))
    return jax.shard_map(
        make_body(mesh.shape["row"] * mesh.shape["col"]),
        mesh=mesh,
        in_specs=(placed,) * 4,
        out_specs=(placed,) * 3,
        check_vma=False,
    )
```

```python
import functools
import math

import jax
import jax.numpy as jnp
from jax import lax
from jax.experimental import pallas as pl
from jax.experimental.pallas import tpu as pltpu
from jax.sharding import PartitionSpec as P

amplitude = 1.0
length_square = 32.0
noise_level = 0.5

AXES = ("row", "col")
LANES = 128
VMEM_BYTES = 32 << 20
PACK_VMEM_BYTES = 63 << 20
RATE = math.log2(math.e) / length_square
SHIFT = math.log2(amplitude)


def in_vmem():
    return pl.BlockSpec(memory_space=pltpu.VMEM)


def halves(values):
    high = values.astype(jnp.bfloat16)
    return high, (values - high.astype(jnp.float32)).astype(jnp.bfloat16)


def narrow(fields, out_ref):
    height = fields.shape[0]
    out_ref[0, :height] = fields[:, :LANES]
    out_ref[0, height:] = jnp.concatenate(
        [fields[: height // 2, LANES:], fields[height // 2 :, LANES:]], axis=1
    )


def pack_kernel(
    points_hbm, direction_hbm, residual_hbm, main_ref, rest_ref, points_ref, direction_ref, residual_ref, arrived
):
    copies = [
        pltpu.make_async_copy(source, target, arrived.at[index])
        for index, (source, target) in enumerate(
            (
                (points_hbm, points_ref),
                (direction_hbm, direction_ref),
                (residual_hbm, residual_ref),
            )
        )
    ]
    for copy in copies:
        copy.start()
    for copy in copies:
        copy.wait()
    direction_high, direction_low = halves(direction_ref[...])
    residual_high, residual_low = halves(residual_ref[...])
    narrow(jnp.concatenate([points_ref[...], direction_high], axis=0), main_ref)
    narrow(jnp.concatenate([residual_high, residual_low, direction_low], axis=0), rest_ref)


def wide(packs):
    height = packs[0].shape[0] * 2 // 3
    side = LANES // 2
    tails = [
        jnp.concatenate([pack[height:, :side], pack[height:, side:]], axis=0) for pack in packs
    ]
    return jnp.concatenate(
        [pack[:height] for pack in packs]
        + [jnp.concatenate(tails[index : index + 2], axis=1) for index in (0, 2)],
        axis=1,
    )


def read(*refs):
    return wide([ref[index] for ref in refs for index in range(ref.shape[0])])


def widened(points, own):
    values = points.astype(jnp.float32)
    half = -0.5 * jnp.sum(values * values, axis=0, keepdims=True)
    high = half.astype(jnp.bfloat16).astype(jnp.float32)
    middle = (half - high).astype(jnp.bfloat16).astype(jnp.float32)
    low = half - high - middle
    row = lax.broadcasted_iota(jnp.int32, (16, points.shape[1]), 0)
    base = 0 if own else 3
    extra = jnp.where(row < 6, 1.0, 0.0)
    extra = jnp.where(row == base, high, extra)
    extra = jnp.where(row == base + 1, middle, extra)
    extra = jnp.where(row == base + 2, low, extra)
    return jnp.concatenate([points, extra.astype(jnp.bfloat16)], axis=0)


def fold(own, piece, applied, dim):
    half = lax.dot_general(
        widened(piece[:dim], False),
        widened(own[:dim], True),
        (((0,), (0,)), ((), ())),
        preferred_element_type=jnp.float32,
    )
    kernel = jnp.exp2(half * RATE + SHIFT).astype(jnp.bfloat16)
    part = lax.dot_general(
        piece[dim:], kernel, (((1,), (0,)), ((), ())), preferred_element_type=jnp.float32
    )
    return part if applied is None else applied + part


def first_fold_kernel(dim, own_ref, beside_ref, rest_ref, applied_ref):
    del beside_ref, rest_ref
    own = read(own_ref)
    applied_ref[...] = fold(own, own, None, dim)


def fold_kernel(dim, own_ref, piece_ref, before_ref, applied_ref):
    applied_ref[...] = fold(read(own_ref), read(piece_ref), before_ref[...], dim)


def join_kernel(first_ref, second_ref, after_ref, joined_ref):
    del after_ref
    count = first_ref.shape[0]
    joined_ref[:count] = first_ref[...]
    joined_ref[count:] = second_ref[...]


def long_fold_kernel(dim, own_ref, piece_ref, before_ref, applied_ref):
    @pl.when(pl.program_id(0) == 0)
    def _():
        applied_ref[...] = before_ref[...]

    applied_ref[...] = fold(read(own_ref), read(piece_ref), applied_ref[...], dim)


def sums_kernel(dim, own_ref, rest_ref, other_rest_ref, applied_ref, sums_ref):
    rest = read(rest_ref, other_rest_ref).astype(jnp.float32)
    probes = rest.shape[0] // 3
    residual = rest[:probes] + rest[probes : 2 * probes]
    direction = read(own_ref)[dim:].astype(jnp.float32) + rest[2 * probes :]
    image = applied_ref[...] + noise_level * direction
    lane = lax.broadcasted_iota(jnp.int32, (image.shape[0], LANES), 1)
    table = jnp.zeros((image.shape[0], LANES), jnp.float32)
    products = (residual * residual, direction * image, residual * image, image * image)
    for index, product in enumerate(products):
        table = jnp.where(lane == index, jnp.sum(product, axis=1, keepdims=True), table)
    sums_ref[...] = table.T[:8]


def last_kernel(dim, own_ref, piece_ref, before_ref, rest_ref, other_rest_ref, applied_ref, sums_ref):
    fold_kernel(dim, own_ref, piece_ref, before_ref, applied_ref)
    sums_kernel(dim, own_ref, rest_ref, other_rest_ref, applied_ref, sums_ref)


def call(kernel, outs, args, folds=0):
    columns, dim, probes = 768, 80, 32
    cost = None
    if folds:
        count = folds * columns * columns
        cost = pl.CostEstimate(
            flops=2 * count * (dim + probes), bytes_accessed=count, transcendentals=count
        )
    return pl.pallas_call(
        kernel,
        out_shape=outs,
        in_specs=[in_vmem()] * len(args),
        out_specs=jax.tree.map(lambda _: in_vmem(), outs),
        compiler_params=pltpu.CompilerParams(vmem_limit_bytes=VMEM_BYTES),
        cost_estimate=cost,
    )(*args)


def pack(points, direction, residual):
    rows = points.shape[0] + direction.shape[0]
    shape = jax.ShapeDtypeStruct((1, rows * 3 // 2, LANES), jnp.bfloat16)
    args = (points, direction, residual)
    return pl.pallas_call(
        pack_kernel,
        out_shape=(shape, shape),
        in_specs=[pl.BlockSpec(memory_space=pltpu.HBM)] * 3,
        out_specs=(in_vmem(), in_vmem()),
        scratch_shapes=[pltpu.VMEM(a.shape, a.dtype) for a in args] + [pltpu.SemaphoreType.DMA((3,))],
        compiler_params=pltpu.CompilerParams(vmem_limit_bytes=PACK_VMEM_BYTES),
    )(*args)


def add_fold(own, piece, before, dim):
    if piece.shape[0] == 4:
        full = jax.ShapeDtypeStruct(before.shape, before.dtype)
        return call(functools.partial(fold_kernel, dim), full, (own, piece, before), 1)
    whole = lambda index: (0, 0)
    return pl.pallas_call(
        functools.partial(long_fold_kernel, dim),
        grid=(piece.shape[0] // 4,),
        out_shape=jax.ShapeDtypeStruct(before.shape, before.dtype),
        in_specs=[
            pl.BlockSpec(own.shape, lambda index: (0, 0, 0)),
            pl.BlockSpec((4, *piece.shape[1:]), lambda index: (index, 0, 0)),
            pl.BlockSpec(before.shape, whole),
        ],
        out_specs=pl.BlockSpec(before.shape, whole),
        compiler_params=pltpu.CompilerParams(vmem_limit_bytes=VMEM_BYTES),
    )(own, piece, before)


def strides(count):
    found = []
    while count > 1:
        assert count % 2 == 0
        count //= 2
        found.append(count)
    return found


def swapped(array, count, stride):
    return lax.ppermute(array, AXES, [(i, i ^ stride) for i in range(count)])


def make_body(count):
    far, middle, near, *others, cores = strides(count)

    def body(points, direction, residual, solution):
        dim, width = points.shape
        probes = direction.shape[0]
        full = jax.ShapeDtypeStruct((probes, 4 * width), jnp.float32)
        table = jax.ShapeDtypeStruct((8, probes), jnp.float32)
        main, rest = pack(points, direction, residual)
        pair = jnp.concatenate([main, swapped(main, count, far)], axis=0)
        rest = jnp.concatenate([rest, swapped(rest, count, far)], axis=0)
        other = swapped(pair, count, middle)
        beside = swapped(pair, count, near)
        other_rest = swapped(rest, count, middle)
        own = jnp.concatenate([pair, other], axis=0)
        other_beside = swapped(other, count, near)
        crossed = swapped(own, count, cores)
        applied = call(functools.partial(first_fold_kernel, dim), full, (own, beside, rest), 1)
        applied = add_fold(own, crossed, applied, dim)
        beside = call(
            join_kernel,
            jax.ShapeDtypeStruct(own.shape, own.dtype),
            (beside, other_beside, applied),
        )
        blocks = [own, beside]
        for stride in others:
            blocks.append(swapped(jnp.concatenate(blocks, axis=0), count, stride))
        for block in blocks[1:]:
            crossed = swapped(block, count, cores)
            applied = add_fold(own, block, applied, dim)
            if block is not blocks[-1]:
                applied = add_fold(own, crossed, applied, dim)
        if crossed.shape[0] == 4:
            applied, sums = call(
                functools.partial(last_kernel, dim),
                (full, table),
                (own, crossed, applied, rest, other_rest),
                1,
            )
        else:
            applied = add_fold(own, crossed, applied, dim)
            sums = call(
                functools.partial(sums_kernel, dim), table, (own, rest, other_rest, applied)
            )
        for stride in (cores, *reversed(others), near):
            sums = sums + swapped(sums, count, stride)
        start = 4 * LANES
        applied = jnp.concatenate([applied[:, :LANES], applied[:, start : start + width - LANES]], axis=1)
        image = applied + noise_level * direction
        old_norm, curvature, cross, image_norm = sums[0], sums[1], sums[2], sums[3]
        step_size = old_norm / curvature
        solution_next = solution + step_size[:, None] * direction
        residual_next = residual - step_size[:, None] * image
        new_norm = old_norm + step_size * (step_size * image_norm - 2.0 * cross)
        direction_next = residual_next + (new_norm / (old_norm + 1e-06))[:, None] * direction
        return (solution_next, residual_next, direction_next)

    return body


def solution(mesh):
    placed = P(None, ("groups", "row", "col"))
    return jax.shard_map(
        make_body(mesh.shape["row"] * mesh.shape["col"]),
        mesh=mesh,
        in_specs=(placed,) * 4,
        out_specs=(placed,) * 3,
        check_vma=False,
    )
```

```python
import functools
import math

import jax
import jax.numpy as jnp
from jax import lax
from jax.experimental import pallas as pl
from jax.experimental.pallas import tpu as pltpu
from jax.sharding import PartitionSpec as P

amplitude = 1.0
length_square = 32.0
noise_level = 0.5

AXES = ("row", "col")
LANES = 128
VMEM_BYTES = 32 << 20
RATE = math.log2(math.e) / length_square
SHIFT = math.log2(amplitude)


def in_vmem():
    return pl.BlockSpec(memory_space=pltpu.VMEM)


def pack_kernel(
    points_hbm, direction_hbm, residual_hbm, packed_ref, points_ref, direction_ref, residual_ref, arrived
):
    copies = [
        pltpu.make_async_copy(source, target, arrived.at[index])
        for index, (source, target) in enumerate(
            (
                (points_hbm, points_ref),
                (direction_hbm, direction_ref),
                (residual_hbm, residual_ref),
            )
        )
    ]
    for copy in copies:
        copy.start()
    for copy in copies:
        copy.wait()
    fields = jnp.concatenate(
        [
            points_ref[...],
            direction_ref[...].astype(jnp.bfloat16),
            residual_ref[...].astype(jnp.bfloat16),
        ],
        axis=0,
    )
    height = fields.shape[0]
    packed_ref[0, :height] = fields[:, :LANES]
    packed_ref[0, height:] = jnp.concatenate(
        [fields[: height // 2, LANES:], fields[height // 2 :, LANES:]], axis=1
    )


def unpack_kernel(packs_ref, held_ref, residual_ref):
    height = packs_ref.shape[1] * 2 // 3
    side = LANES // 2
    first, second = packs_ref[0, height:], packs_ref[1, height:]
    tails = jnp.concatenate(
        [
            jnp.concatenate([first[:, :side], second[:, :side]], axis=1),
            jnp.concatenate([first[:, side:], second[:, side:]], axis=1),
        ],
        axis=0,
    )
    rows = held_ref.shape[1]
    for index, part in enumerate((packs_ref[0, :height], packs_ref[1, :height], tails)):
        span = slice(index * LANES, (index + 1) * LANES)
        held_ref[0, :, span] = part[:rows]
        residual_ref[:, span] = part[rows:].astype(jnp.float32)


def read(ref):
    return jnp.concatenate([ref[index] for index in range(ref.shape[0])], axis=1)


def widened(points, own):
    values = points.astype(jnp.float32)
    half = -0.5 * jnp.sum(values * values, axis=0, keepdims=True)
    high = half.astype(jnp.bfloat16).astype(jnp.float32)
    middle = (half - high).astype(jnp.bfloat16).astype(jnp.float32)
    low = half - high - middle
    row = lax.broadcasted_iota(jnp.int32, (16, points.shape[1]), 0)
    base = 0 if own else 3
    extra = jnp.where(row < 6, 1.0, 0.0)
    extra = jnp.where(row == base, high, extra)
    extra = jnp.where(row == base + 1, middle, extra)
    extra = jnp.where(row == base + 2, low, extra)
    return jnp.concatenate([points, extra.astype(jnp.bfloat16)], axis=0)


def fold(own, piece, applied, dim):
    half = lax.dot_general(
        widened(piece[:dim], False),
        widened(own[:dim], True),
        (((0,), (0,)), ((), ())),
        preferred_element_type=jnp.float32,
    )
    kernel = jnp.exp2(half * RATE + SHIFT).astype(jnp.bfloat16)
    part = lax.dot_general(
        piece[dim:], kernel, (((1,), (0,)), ((), ())), preferred_element_type=jnp.float32
    )
    return part if applied is None else applied + part


def first_fold_kernel(dim, own_ref, applied_ref):
    own = read(own_ref)
    applied_ref[...] = fold(own, own, None, dim)


def fold_kernel(dim, own_ref, piece_ref, before_ref, applied_ref):
    applied_ref[...] = fold(read(own_ref), read(piece_ref), before_ref[...], dim)


def join_kernel(first_ref, after_ref, joined_ref):
    del after_ref
    joined_ref[...] = first_ref[...]


def long_fold_kernel(dim, own_ref, piece_ref, before_ref, applied_ref):
    @pl.when(pl.program_id(0) == 0)
    def _():
        applied_ref[...] = before_ref[...]

    applied_ref[...] = fold(read(own_ref), read(piece_ref), applied_ref[...], dim)


def sums_kernel(dim, own_ref, residual_ref, other_residual_ref, applied_ref, sums_ref):
    residual = jnp.concatenate([residual_ref[...], other_residual_ref[...]], axis=1)
    direction = read(own_ref)[dim:].astype(jnp.float32)
    image = applied_ref[...] + noise_level * direction
    lane = lax.broadcasted_iota(jnp.int32, (image.shape[0], LANES), 1)
    table = jnp.zeros((image.shape[0], LANES), jnp.float32)
    products = (residual * residual, direction * image, residual * image, image * image)
    for index, product in enumerate(products):
        table = jnp.where(lane == index, jnp.sum(product, axis=1, keepdims=True), table)
    sums_ref[...] = table.T[:8]


def last_kernel(dim, own_ref, piece_ref, before_ref, residual_ref, other_residual_ref, applied_ref, sums_ref):
    fold_kernel(dim, own_ref, piece_ref, before_ref, applied_ref)
    sums_kernel(dim, own_ref, residual_ref, other_residual_ref, applied_ref, sums_ref)


def call(kernel, outs, args, folds=0):
    columns, dim, probes = 768, 80, 32
    cost = None
    if folds:
        count = folds * columns * columns
        cost = pl.CostEstimate(
            flops=2 * count * (dim + probes), bytes_accessed=count, transcendentals=count
        )
    return pl.pallas_call(
        kernel,
        out_shape=outs,
        in_specs=[in_vmem()] * len(args),
        out_specs=jax.tree.map(lambda _: in_vmem(), outs),
        compiler_params=pltpu.CompilerParams(vmem_limit_bytes=VMEM_BYTES),
        cost_estimate=cost,
    )(*args)


def pack(points, direction, residual):
    rows = points.shape[0] + direction.shape[0] + residual.shape[0]
    shape = pltpu.VMEM((1, rows * 3 // 2, LANES), jnp.bfloat16)
    args = [pltpu.with_memory_space_constraint(a, pltpu.HBM) for a in (points, direction, residual)]
    return pl.pallas_call(
        pack_kernel,
        out_shape=shape,
        in_specs=[pl.BlockSpec(memory_space=pltpu.HBM)] * 3,
        out_specs=in_vmem(),
        scratch_shapes=[pltpu.VMEM(a.shape, a.dtype) for a in args] + [pltpu.SemaphoreType.DMA((3,))],
        compiler_params=pltpu.CompilerParams(vmem_limit_bytes=VMEM_BYTES),
    )(*args)


def unpack(packs, dim, probes):
    columns = 3 * LANES
    outs = (
        jax.ShapeDtypeStruct((1, dim + probes, columns), packs.dtype),
        jax.ShapeDtypeStruct((probes, columns), jnp.float32),
    )
    return call(unpack_kernel, outs, (packs,))


def add_fold(own, piece, before, dim):
    if piece.shape[0] == 2:
        full = jax.ShapeDtypeStruct(before.shape, before.dtype)
        return call(functools.partial(fold_kernel, dim), full, (own, piece, before), 1)
    whole = lambda index: (0, 0)
    return pl.pallas_call(
        functools.partial(long_fold_kernel, dim),
        grid=(piece.shape[0] // 2,),
        out_shape=jax.ShapeDtypeStruct(before.shape, before.dtype),
        in_specs=[
            pl.BlockSpec(own.shape, lambda index: (0, 0, 0)),
            pl.BlockSpec((2, *piece.shape[1:]), lambda index: (index, 0, 0)),
            pl.BlockSpec(before.shape, whole),
        ],
        out_specs=pl.BlockSpec(before.shape, whole),
        compiler_params=pltpu.CompilerParams(vmem_limit_bytes=VMEM_BYTES),
    )(own, piece, before)


def strides(count):
    found = []
    while count > 1:
        assert count % 2 == 0
        count //= 2
        found.append(count)
    return found


def swapped(array, count, stride):
    return lax.ppermute(array, AXES, [(i, i ^ stride) for i in range(count)])


def make_body(count):
    far, middle, near, *others, cores = strides(count)

    def body(points, direction, residual, solution):
        dim, width = points.shape
        probes = direction.shape[0]
        full = jax.ShapeDtypeStruct((probes, 4 * width), jnp.float32)
        table = jax.ShapeDtypeStruct((8, probes), jnp.float32)
        packed = pack(points, direction, residual)
        pair = jnp.concatenate([packed, swapped(packed, count, far)], axis=0)
        other = swapped(pair, count, middle)
        half, rest = unpack(pair, dim, probes)
        other_half, other_rest = unpack(other, dim, probes)
        own = jnp.concatenate([half, other_half], axis=0)
        beside = swapped(half, count, near)
        other_beside = swapped(other_half, count, near)
        crossed = swapped(own, count, cores)
        applied = call(functools.partial(first_fold_kernel, dim), full, (own,), 1)
        applied = add_fold(own, crossed, applied, dim)
        beside = call(
            join_kernel,
            jax.ShapeDtypeStruct(own.shape, own.dtype),
            (jnp.concatenate([beside, other_beside], axis=0), applied),
        )
        blocks = [own, beside]
        for stride in others:
            blocks.append(swapped(jnp.concatenate(blocks, axis=0), count, stride))
        for block in blocks[1:]:
            crossed = swapped(block, count, cores)
            applied = add_fold(own, block, applied, dim)
            if block is not blocks[-1]:
                applied = add_fold(own, crossed, applied, dim)
        if crossed.shape[0] == 2:
            applied, sums = call(
                functools.partial(last_kernel, dim),
                (full, table),
                (own, crossed, applied, rest, other_rest),
                1,
            )
        else:
            applied = add_fold(own, crossed, applied, dim)
            sums = call(
                functools.partial(sums_kernel, dim), table, (own, rest, other_rest, applied)
            )
        for stride in (cores, *reversed(others), near):
            sums = sums + swapped(sums, count, stride)
        start = 2 * LANES
        applied = jnp.concatenate([applied[:, :LANES], applied[:, start : start + width - LANES]], axis=1)
        image = applied + noise_level * direction
        old_norm, curvature, cross, image_norm = sums[0], sums[1], sums[2], sums[3]
        step_size = old_norm / curvature
        solution_next = solution + step_size[:, None] * direction
        residual_next = residual - step_size[:, None] * image
        new_norm = old_norm + step_size * (step_size * image_norm - 2.0 * cross)
        direction_next = residual_next + (new_norm / (old_norm + 1e-06))[:, None] * direction
        return (solution_next, residual_next, direction_next)

    return body


def solution(mesh):
    placed = P(None, ("groups", "row", "col"))
    return jax.shard_map(
        make_body(mesh.shape["row"] * mesh.shape["col"]),
        mesh=mesh,
        in_specs=(placed,) * 4,
        out_specs=(placed,) * 3,
        check_vma=False,
    )
```

```python
import functools
import math

import jax
import jax.numpy as jnp
from jax import lax
from jax.experimental import pallas as pl
from jax.experimental.pallas import tpu as pltpu
from jax.sharding import PartitionSpec as P

amplitude = 1.0
length_square = 32.0
noise_level = 0.5

AXES = ("row", "col")
LANES = 128
VMEM_BYTES = 32 << 20
RATE = math.log2(math.e) / length_square
SHIFT = math.log2(amplitude)


def in_vmem():
    return pl.BlockSpec(memory_space=pltpu.VMEM)


def pack_kernel(
    points_hbm, direction_hbm, residual_hbm, packed_ref, points_ref, direction_ref, residual_ref, arrived
):
    copies = [
        pltpu.make_async_copy(source, target, arrived.at[index])
        for index, (source, target) in enumerate(
            (
                (points_hbm, points_ref),
                (direction_hbm, direction_ref),
                (residual_hbm, residual_ref),
            )
        )
    ]
    for copy in copies:
        copy.start()
    for copy in copies:
        copy.wait()
    fields = jnp.concatenate(
        [
            points_ref[...],
            direction_ref[...].astype(jnp.bfloat16),
            residual_ref[...].astype(jnp.bfloat16),
        ],
        axis=0,
    )
    height = fields.shape[0]
    packed_ref[0, :height] = fields[:, :LANES]
    packed_ref[0, height:] = jnp.concatenate(
        [fields[: height // 2, LANES:], fields[height // 2 :, LANES:]], axis=1
    )


def unpack_kernel(packs_ref, held_ref, residual_ref):
    height = packs_ref.shape[1] * 2 // 3
    side = LANES // 2
    first, second = packs_ref[0, height:], packs_ref[1, height:]
    tails = jnp.concatenate(
        [
            jnp.concatenate([first[:, :side], second[:, :side]], axis=1),
            jnp.concatenate([first[:, side:], second[:, side:]], axis=1),
        ],
        axis=0,
    )
    rows = held_ref.shape[1]
    for index, part in enumerate((packs_ref[0, :height], packs_ref[1, :height], tails)):
        span = slice(index * LANES, (index + 1) * LANES)
        held_ref[0, :, span] = part[:rows]
        residual_ref[:, span] = part[rows:].astype(jnp.float32)


def read(ref):
    return jnp.concatenate([ref[index] for index in range(ref.shape[0])], axis=1)


def widened(points, own):
    values = points.astype(jnp.float32)
    half = -0.5 * jnp.sum(values * values, axis=0, keepdims=True)
    high = half.astype(jnp.bfloat16).astype(jnp.float32)
    middle = (half - high).astype(jnp.bfloat16).astype(jnp.float32)
    low = half - high - middle
    row = lax.broadcasted_iota(jnp.int32, (16, points.shape[1]), 0)
    base = 0 if own else 3
    extra = jnp.where(row < 6, 1.0, 0.0)
    extra = jnp.where(row == base, high, extra)
    extra = jnp.where(row == base + 1, middle, extra)
    extra = jnp.where(row == base + 2, low, extra)
    return jnp.concatenate([points, extra.astype(jnp.bfloat16)], axis=0)


def fold(own, piece, applied, dim):
    half = lax.dot_general(
        widened(piece[:dim], False),
        widened(own[:dim], True),
        (((0,), (0,)), ((), ())),
        preferred_element_type=jnp.float32,
    )
    kernel = jnp.exp2(half * RATE + SHIFT).astype(jnp.bfloat16)
    part = lax.dot_general(
        piece[dim:], kernel, (((1,), (0,)), ((), ())), preferred_element_type=jnp.float32
    )
    return part if applied is None else applied + part


def first_fold_kernel(dim, own_ref, applied_ref):
    own = read(own_ref)
    applied_ref[...] = fold(own, own, None, dim)


def fold_kernel(dim, own_ref, piece_ref, before_ref, applied_ref):
    applied_ref[...] = fold(read(own_ref), read(piece_ref), before_ref[...], dim)


def join_kernel(first_ref, second_ref, after_ref, joined_ref):
    del after_ref
    count = first_ref.shape[0]
    joined_ref[:count] = first_ref[...]
    joined_ref[count:] = second_ref[...]


def long_fold_kernel(dim, own_ref, piece_ref, before_ref, applied_ref):
    @pl.when(pl.program_id(0) == 0)
    def _():
        applied_ref[...] = before_ref[...]

    applied_ref[...] = fold(read(own_ref), read(piece_ref), applied_ref[...], dim)


def sums_kernel(dim, own_ref, residual_ref, other_residual_ref, applied_ref, sums_ref):
    residual = jnp.concatenate([residual_ref[...], other_residual_ref[...]], axis=1)
    direction = read(own_ref)[dim:].astype(jnp.float32)
    image = applied_ref[...] + noise_level * direction
    lane = lax.broadcasted_iota(jnp.int32, (image.shape[0], LANES), 1)
    table = jnp.zeros((image.shape[0], LANES), jnp.float32)
    products = (residual * residual, direction * image, residual * image, image * image)
    for index, product in enumerate(products):
        table = jnp.where(lane == index, jnp.sum(product, axis=1, keepdims=True), table)
    sums_ref[...] = table.T[:8]


def last_kernel(dim, own_ref, piece_ref, before_ref, residual_ref, other_residual_ref, applied_ref, sums_ref):
    fold_kernel(dim, own_ref, piece_ref, before_ref, applied_ref)
    sums_kernel(dim, own_ref, residual_ref, other_residual_ref, applied_ref, sums_ref)


def call(kernel, outs, args, folds=0):
    columns, dim, probes = 768, 80, 32
    cost = None
    if folds:
        count = folds * columns * columns
        cost = pl.CostEstimate(
            flops=2 * count * (dim + probes), bytes_accessed=count, transcendentals=count
        )
    return pl.pallas_call(
        kernel,
        out_shape=outs,
        in_specs=[in_vmem()] * len(args),
        out_specs=jax.tree.map(lambda _: in_vmem(), outs),
        compiler_params=pltpu.CompilerParams(vmem_limit_bytes=VMEM_BYTES),
        cost_estimate=cost,
    )(*args)


def pack(points, direction, residual):
    rows = points.shape[0] + direction.shape[0] + residual.shape[0]
    shape = pltpu.VMEM((1, rows * 3 // 2, LANES), jnp.bfloat16)
    args = [pltpu.with_memory_space_constraint(a, pltpu.HBM) for a in (points, direction, residual)]
    return pl.pallas_call(
        pack_kernel,
        out_shape=shape,
        in_specs=[pl.BlockSpec(memory_space=pltpu.HBM)] * 3,
        out_specs=in_vmem(),
        scratch_shapes=[pltpu.VMEM(a.shape, a.dtype) for a in args] + [pltpu.SemaphoreType.DMA((3,))],
        compiler_params=pltpu.CompilerParams(vmem_limit_bytes=VMEM_BYTES),
    )(*args)


def unpack(packs, dim, probes):
    columns = 3 * LANES
    outs = (
        jax.ShapeDtypeStruct((1, dim + probes, columns), packs.dtype),
        jax.ShapeDtypeStruct((probes, columns), jnp.float32),
    )
    return call(unpack_kernel, outs, (packs,))


def add_fold(own, piece, before, dim):
    if piece.shape[0] == 2:
        full = jax.ShapeDtypeStruct(before.shape, before.dtype)
        return call(functools.partial(fold_kernel, dim), full, (own, piece, before), 1)
    whole = lambda index: (0, 0)
    return pl.pallas_call(
        functools.partial(long_fold_kernel, dim),
        grid=(piece.shape[0] // 2,),
        out_shape=jax.ShapeDtypeStruct(before.shape, before.dtype),
        in_specs=[
            pl.BlockSpec(own.shape, lambda index: (0, 0, 0)),
            pl.BlockSpec((2, *piece.shape[1:]), lambda index: (index, 0, 0)),
            pl.BlockSpec(before.shape, whole),
        ],
        out_specs=pl.BlockSpec(before.shape, whole),
        compiler_params=pltpu.CompilerParams(vmem_limit_bytes=VMEM_BYTES),
    )(own, piece, before)


def strides(count):
    found = []
    while count > 1:
        assert count % 2 == 0
        count //= 2
        found.append(count)
    return found


def swapped(array, count, stride):
    return lax.ppermute(array, AXES, [(i, i ^ stride) for i in range(count)])


def make_body(count):
    far, middle, near, *others, cores = strides(count)

    def body(points, direction, residual, solution):
        dim, width = points.shape
        probes = direction.shape[0]
        full = jax.ShapeDtypeStruct((probes, 4 * width), jnp.float32)
        table = jax.ShapeDtypeStruct((8, probes), jnp.float32)
        packed = pack(points, direction, residual)
        pair = jnp.concatenate([packed, swapped(packed, count, far)], axis=0)
        other = swapped(pair, count, middle)
        half, rest = unpack(pair, dim, probes)
        other_half, other_rest = unpack(other, dim, probes)
        own = jnp.concatenate([half, other_half], axis=0)
        beside = swapped(half, count, near)
        other_beside = swapped(half, count, near | middle)
        crossed = swapped(own, count, cores)
        applied = call(functools.partial(first_fold_kernel, dim), full, (own,), 1)
        beside = call(
            join_kernel,
            jax.ShapeDtypeStruct(own.shape, own.dtype),
            (beside, other_beside, applied),
        )
        applied = add_fold(own, crossed, applied, dim)
        blocks = [own, beside]
        for stride in others:
            blocks.append(swapped(jnp.concatenate(blocks, axis=0), count, stride))
        for block in blocks[1:]:
            crossed = swapped(block, count, cores)
            applied = add_fold(own, block, applied, dim)
            if block is not blocks[-1]:
                applied = add_fold(own, crossed, applied, dim)
        if crossed.shape[0] == 2:
            applied, sums = call(
                functools.partial(last_kernel, dim),
                (full, table),
                (own, crossed, applied, rest, other_rest),
                1,
            )
        else:
            applied = add_fold(own, crossed, applied, dim)
            sums = call(
                functools.partial(sums_kernel, dim), table, (own, rest, other_rest, applied)
            )
        for stride in (cores, *reversed(others), near):
            sums = sums + swapped(sums, count, stride)
        start = 2 * LANES
        applied = jnp.concatenate([applied[:, :LANES], applied[:, start : start + width - LANES]], axis=1)
        image = applied + noise_level * direction
        old_norm, curvature, cross, image_norm = sums[0], sums[1], sums[2], sums[3]
        step_size = old_norm / curvature
        solution_next = solution + step_size[:, None] * direction
        residual_next = residual - step_size[:, None] * image
        new_norm = old_norm + step_size * (step_size * image_norm - 2.0 * cross)
        direction_next = residual_next + (new_norm / (old_norm + 1e-06))[:, None] * direction
        return (solution_next, residual_next, direction_next)

    return body


def solution(mesh):
    placed = P(None, ("groups", "row", "col"))
    return jax.shard_map(
        make_body(mesh.shape["row"] * mesh.shape["col"]),
        mesh=mesh,
        in_specs=(placed,) * 4,
        out_specs=(placed,) * 3,
        check_vma=False,
    )
```

```python
import functools
import math

import jax
import jax.numpy as jnp
from jax import lax
from jax.experimental import pallas as pl
from jax.experimental.pallas import tpu as pltpu
from jax.sharding import PartitionSpec as P

amplitude = 1.0
length_square = 32.0
noise_level = 0.5

AXES = ("row", "col")
LANES = 128
VMEM_BYTES = 32 << 20
RATE = math.log2(math.e) / length_square
SHIFT = math.log2(amplitude)


def in_vmem():
    return pl.BlockSpec(memory_space=pltpu.VMEM)


def pack_kernel(
    points_hbm, direction_hbm, residual_hbm, packed_ref, points_ref, direction_ref, residual_ref, arrived
):
    copies = [
        pltpu.make_async_copy(source, target, arrived.at[index])
        for index, (source, target) in enumerate(
            (
                (points_hbm, points_ref),
                (direction_hbm, direction_ref),
                (residual_hbm, residual_ref),
            )
        )
    ]
    for copy in copies:
        copy.start()
    for copy in copies:
        copy.wait()
    fields = jnp.concatenate(
        [
            points_ref[...],
            direction_ref[...].astype(jnp.bfloat16),
            residual_ref[...].astype(jnp.bfloat16),
        ],
        axis=0,
    )
    height = fields.shape[0]
    packed_ref[0, :height] = fields[:, :LANES]
    packed_ref[0, height:] = jnp.concatenate(
        [fields[: height // 2, LANES:], fields[height // 2 :, LANES:]], axis=1
    )


def unpack_kernel(packs_ref, held_ref, residual_ref):
    height = packs_ref.shape[1] * 2 // 3
    side = LANES // 2
    first, second = packs_ref[0, height:], packs_ref[1, height:]
    tails = jnp.concatenate(
        [
            jnp.concatenate([first[:, :side], second[:, :side]], axis=1),
            jnp.concatenate([first[:, side:], second[:, side:]], axis=1),
        ],
        axis=0,
    )
    rows = held_ref.shape[1]
    for index, part in enumerate((packs_ref[0, :height], packs_ref[1, :height], tails)):
        span = slice(index * LANES, (index + 1) * LANES)
        held_ref[0, :, span] = part[:rows]
        residual_ref[:, span] = part[rows:].astype(jnp.float32)


def read(ref):
    return jnp.concatenate([ref[index] for index in range(ref.shape[0])], axis=1)


def widened(points, own):
    values = points.astype(jnp.float32)
    half = -0.5 * jnp.sum(values * values, axis=0, keepdims=True)
    high = half.astype(jnp.bfloat16).astype(jnp.float32)
    middle = (half - high).astype(jnp.bfloat16).astype(jnp.float32)
    low = half - high - middle
    row = lax.broadcasted_iota(jnp.int32, (16, points.shape[1]), 0)
    base = 0 if own else 3
    extra = jnp.where(row < 6, 1.0, 0.0)
    extra = jnp.where(row == base, high, extra)
    extra = jnp.where(row == base + 1, middle, extra)
    extra = jnp.where(row == base + 2, low, extra)
    return jnp.concatenate([points, extra.astype(jnp.bfloat16)], axis=0)


def fold(own, piece, applied, dim):
    half = lax.dot_general(
        widened(piece[:dim], False),
        widened(own[:dim], True),
        (((0,), (0,)), ((), ())),
        preferred_element_type=jnp.float32,
    )
    kernel = jnp.exp2(half * RATE + SHIFT).astype(jnp.bfloat16)
    part = lax.dot_general(
        piece[dim:], kernel, (((1,), (0,)), ((), ())), preferred_element_type=jnp.float32
    )
    return part if applied is None else applied + part


def first_fold_kernel(dim, own_ref, applied_ref):
    own = read(own_ref)
    applied_ref[...] = fold(own, own, None, dim)


def fold_kernel(dim, own_ref, piece_ref, before_ref, applied_ref):
    applied_ref[...] = fold(read(own_ref), read(piece_ref), before_ref[...], dim)


def join_kernel(first_ref, second_ref, after_ref, joined_ref):
    del after_ref
    count = first_ref.shape[0]
    joined_ref[:count] = first_ref[...]
    joined_ref[count:] = second_ref[...]


def long_fold_kernel(dim, own_ref, piece_ref, before_ref, applied_ref):
    @pl.when(pl.program_id(0) == 0)
    def _():
        applied_ref[...] = before_ref[...]

    applied_ref[...] = fold(read(own_ref), read(piece_ref), applied_ref[...], dim)


def sums_kernel(dim, own_ref, residual_ref, other_residual_ref, applied_ref, sums_ref):
    residual = jnp.concatenate([residual_ref[...], other_residual_ref[...]], axis=1)
    direction = read(own_ref)[dim:].astype(jnp.float32)
    image = applied_ref[...] + noise_level * direction
    lane = lax.broadcasted_iota(jnp.int32, (image.shape[0], LANES), 1)
    table = jnp.zeros((image.shape[0], LANES), jnp.float32)
    products = (residual * residual, direction * image, residual * image, image * image)
    for index, product in enumerate(products):
        table = jnp.where(lane == index, jnp.sum(product, axis=1, keepdims=True), table)
    sums_ref[...] = table.T[:8]


def last_kernel(dim, own_ref, piece_ref, before_ref, residual_ref, other_residual_ref, applied_ref, sums_ref):
    fold_kernel(dim, own_ref, piece_ref, before_ref, applied_ref)
    sums_kernel(dim, own_ref, residual_ref, other_residual_ref, applied_ref, sums_ref)


def call(kernel, outs, args, folds=0):
    columns, dim, probes = 768, 80, 32
    cost = None
    if folds:
        count = folds * columns * columns
        cost = pl.CostEstimate(
            flops=2 * count * (dim + probes), bytes_accessed=count, transcendentals=count
        )
    return pl.pallas_call(
        kernel,
        out_shape=outs,
        in_specs=[in_vmem()] * len(args),
        out_specs=jax.tree.map(lambda _: in_vmem(), outs),
        compiler_params=pltpu.CompilerParams(vmem_limit_bytes=VMEM_BYTES),
        cost_estimate=cost,
    )(*args)


def pack(points, direction, residual):
    rows = points.shape[0] + direction.shape[0] + residual.shape[0]
    shape = pltpu.VMEM((1, rows * 3 // 2, LANES), jnp.bfloat16)
    args = [pltpu.with_memory_space_constraint(a, pltpu.HBM) for a in (points, direction, residual)]
    return pl.pallas_call(
        pack_kernel,
        out_shape=shape,
        in_specs=[pl.BlockSpec(memory_space=pltpu.HBM)] * 3,
        out_specs=in_vmem(),
        scratch_shapes=[pltpu.VMEM(a.shape, a.dtype) for a in args] + [pltpu.SemaphoreType.DMA((3,))],
        compiler_params=pltpu.CompilerParams(vmem_limit_bytes=VMEM_BYTES),
    )(*args)


def unpack(packs, dim, probes):
    columns = 3 * LANES
    outs = (
        jax.ShapeDtypeStruct((1, dim + probes, columns), packs.dtype),
        jax.ShapeDtypeStruct((probes, columns), jnp.float32),
    )
    return call(unpack_kernel, outs, (packs,))


def add_fold(own, piece, before, dim):
    if piece.shape[0] == 2:
        full = jax.ShapeDtypeStruct(before.shape, before.dtype)
        return call(functools.partial(fold_kernel, dim), full, (own, piece, before), 1)
    whole = lambda index: (0, 0)
    return pl.pallas_call(
        functools.partial(long_fold_kernel, dim),
        grid=(piece.shape[0] // 2,),
        out_shape=jax.ShapeDtypeStruct(before.shape, before.dtype),
        in_specs=[
            pl.BlockSpec(own.shape, lambda index: (0, 0, 0)),
            pl.BlockSpec((2, *piece.shape[1:]), lambda index: (index, 0, 0)),
            pl.BlockSpec(before.shape, whole),
        ],
        out_specs=pl.BlockSpec(before.shape, whole),
        compiler_params=pltpu.CompilerParams(vmem_limit_bytes=VMEM_BYTES),
    )(own, piece, before)


def strides(count):
    found = []
    while count > 1:
        assert count % 2 == 0
        count //= 2
        found.append(count)
    return found


def swapped(array, count, stride):
    return lax.ppermute(array, AXES, [(i, i ^ stride) for i in range(count)])


def make_body(count):
    far, middle, near, *others, cores = strides(count)

    def body(points, direction, residual, solution):
        dim, width = points.shape
        probes = direction.shape[0]
        full = jax.ShapeDtypeStruct((probes, 4 * width), jnp.float32)
        table = jax.ShapeDtypeStruct((8, probes), jnp.float32)
        packed = pack(points, direction, residual)
        pair = jnp.concatenate([packed, swapped(packed, count, far)], axis=0)
        other = swapped(pair, count, middle)
        half, rest = unpack(pair, dim, probes)
        other_half, other_rest = unpack(other, dim, probes)
        own = jnp.concatenate([half, other_half], axis=0)
        beside = swapped(half, count, near)
        other_beside = swapped(half, count, near | middle)
        crossed = swapped(own, count, cores)
        applied = call(functools.partial(first_fold_kernel, dim), full, (own,), 1)
        beside = call(
            join_kernel,
            jax.ShapeDtypeStruct(own.shape, own.dtype),
            (beside, other_beside, applied),
        )
        applied = add_fold(own, crossed, applied, dim)
        blocks = [own, beside]
        for stride in others:
            blocks.append(swapped(jnp.concatenate(blocks, axis=0), count, stride))
        for block in blocks[1:]:
            crossed = swapped(block, count, cores)
            applied = add_fold(own, block, applied, dim)
            if block is not blocks[-1]:
                applied = add_fold(own, crossed, applied, dim)
        if crossed.shape[0] == 2:
            applied, sums = call(
                functools.partial(last_kernel, dim),
                (full, table),
                (own, crossed, applied, rest, other_rest),
                1,
            )
        else:
            applied = add_fold(own, crossed, applied, dim)
            sums = call(
                functools.partial(sums_kernel, dim), table, (own, rest, other_rest, applied)
            )
        for stride in others:
            sums = sums + swapped(sums, count, stride)
        sums = (
            sums
            + swapped(sums, count, near)
            + swapped(sums, count, near | cores)
            + swapped(sums, count, cores)
        )
        start = 2 * LANES
        applied = jnp.concatenate([applied[:, :LANES], applied[:, start : start + width - LANES]], axis=1)
        image = applied + noise_level * direction
        old_norm, curvature, cross, image_norm = sums[0], sums[1], sums[2], sums[3]
        step_size = old_norm / curvature
        solution_next = solution + step_size[:, None] * direction
        residual_next = residual - step_size[:, None] * image
        new_norm = old_norm + step_size * (step_size * image_norm - 2.0 * cross)
        direction_next = residual_next + (new_norm / (old_norm + 1e-06))[:, None] * direction
        return (solution_next, residual_next, direction_next)

    return body


def solution(mesh):
    placed = P(None, ("groups", "row", "col"))
    return jax.shard_map(
        make_body(mesh.shape["row"] * mesh.shape["col"]),
        mesh=mesh,
        in_specs=(placed,) * 4,
        out_specs=(placed,) * 3,
        check_vma=False,
    )
```

```python
import functools
import math

import jax
import jax.numpy as jnp
from jax import lax
from jax.experimental import pallas as pl
from jax.experimental.pallas import tpu as pltpu
from jax.sharding import PartitionSpec as P

amplitude = 1.0
length_square = 32.0
noise_level = 0.5

AXES = ("row", "col")
LANES = 128
VMEM_BYTES = 32 << 20
RATE = math.log2(math.e) / length_square
SHIFT = math.log2(amplitude)


def in_vmem():
    return pl.BlockSpec(memory_space=pltpu.VMEM)


def pack_kernel(
    points_hbm, direction_hbm, residual_hbm, packed_ref, points_ref, direction_ref, residual_ref, arrived
):
    copies = [
        pltpu.make_async_copy(source, target, arrived.at[index])
        for index, (source, target) in enumerate(
            (
                (points_hbm, points_ref),
                (direction_hbm, direction_ref),
                (residual_hbm, residual_ref),
            )
        )
    ]
    for copy in copies:
        copy.start()
    for copy in copies:
        copy.wait()
    fields = jnp.concatenate(
        [
            points_ref[...],
            direction_ref[...].astype(jnp.bfloat16),
            residual_ref[...].astype(jnp.bfloat16),
        ],
        axis=0,
    )
    height = fields.shape[0]
    packed_ref[0, :height] = fields[:, :LANES]
    packed_ref[0, height:] = jnp.concatenate(
        [fields[: height // 2, LANES:], fields[height // 2 :, LANES:]], axis=1
    )


def unpack_kernel(packs_ref, held_ref, residual_ref):
    height = packs_ref.shape[1] * 2 // 3
    side = LANES // 2
    first, second = packs_ref[0, height:], packs_ref[1, height:]
    tails = jnp.concatenate(
        [
            jnp.concatenate([first[:, :side], second[:, :side]], axis=1),
            jnp.concatenate([first[:, side:], second[:, side:]], axis=1),
        ],
        axis=0,
    )
    rows = held_ref.shape[1]
    for index, part in enumerate((packs_ref[0, :height], packs_ref[1, :height], tails)):
        span = slice(index * LANES, (index + 1) * LANES)
        held_ref[0, :, span] = part[:rows]
        residual_ref[:, span] = part[rows:].astype(jnp.float32)


def read(ref):
    return jnp.concatenate([ref[index] for index in range(ref.shape[0])], axis=1)


def widened(points, own):
    values = points.astype(jnp.float32)
    half = -0.5 * jnp.sum(values * values, axis=0, keepdims=True)
    high = half.astype(jnp.bfloat16).astype(jnp.float32)
    middle = (half - high).astype(jnp.bfloat16).astype(jnp.float32)
    low = half - high - middle
    row = lax.broadcasted_iota(jnp.int32, (16, points.shape[1]), 0)
    base = 0 if own else 3
    extra = jnp.where(row < 6, 1.0, 0.0)
    extra = jnp.where(row == base, high, extra)
    extra = jnp.where(row == base + 1, middle, extra)
    extra = jnp.where(row == base + 2, low, extra)
    return jnp.concatenate([points, extra.astype(jnp.bfloat16)], axis=0)


def fold(own, piece, applied, dim):
    half = lax.dot_general(
        widened(piece[:dim], False),
        widened(own[:dim], True),
        (((0,), (0,)), ((), ())),
        preferred_element_type=jnp.float32,
    )
    kernel = jnp.exp2(half * RATE + SHIFT).astype(jnp.bfloat16)
    part = lax.dot_general(
        piece[dim:], kernel, (((1,), (0,)), ((), ())), preferred_element_type=jnp.float32
    )
    return part if applied is None else applied + part


def first_fold_kernel(dim, own_ref, applied_ref):
    own = read(own_ref)
    applied_ref[...] = fold(own, own, None, dim)


def fold_kernel(dim, own_ref, piece_ref, before_ref, applied_ref):
    applied_ref[...] = fold(read(own_ref), read(piece_ref), before_ref[...], dim)


def join_kernel(first_ref, second_ref, after_ref, joined_ref):
    del after_ref
    count = first_ref.shape[0]
    joined_ref[:count] = first_ref[...]
    joined_ref[count:] = second_ref[...]


def long_fold_kernel(dim, own_ref, piece_ref, before_ref, applied_ref):
    @pl.when(pl.program_id(0) == 0)
    def _():
        applied_ref[...] = before_ref[...]

    applied_ref[...] = fold(read(own_ref), read(piece_ref), applied_ref[...], dim)


def sums_kernel(dim, own_ref, residual_ref, other_residual_ref, applied_ref, sums_ref):
    residual = jnp.concatenate([residual_ref[...], other_residual_ref[...]], axis=1)
    direction = read(own_ref)[dim:].astype(jnp.float32)
    image = applied_ref[...] + noise_level * direction
    lane = lax.broadcasted_iota(jnp.int32, (image.shape[0], LANES), 1)
    table = jnp.zeros((image.shape[0], LANES), jnp.float32)
    products = (residual * residual, direction * image, residual * image, image * image)
    for index, product in enumerate(products):
        table = jnp.where(lane == index, jnp.sum(product, axis=1, keepdims=True), table)
    sums_ref[...] = table.T[:8]


def last_kernel(dim, own_ref, piece_ref, before_ref, residual_ref, other_residual_ref, applied_ref, sums_ref):
    fold_kernel(dim, own_ref, piece_ref, before_ref, applied_ref)
    sums_kernel(dim, own_ref, residual_ref, other_residual_ref, applied_ref, sums_ref)


def call(kernel, outs, args, folds=0):
    columns, dim, probes = 768, 80, 32
    cost = None
    if folds:
        count = folds * columns * columns
        cost = pl.CostEstimate(
            flops=2 * count * (dim + probes), bytes_accessed=count, transcendentals=count
        )
    return pl.pallas_call(
        kernel,
        out_shape=outs,
        in_specs=[in_vmem()] * len(args),
        out_specs=jax.tree.map(lambda _: in_vmem(), outs),
        compiler_params=pltpu.CompilerParams(vmem_limit_bytes=VMEM_BYTES),
        cost_estimate=cost,
    )(*args)


def pack(points, direction, residual):
    rows = points.shape[0] + direction.shape[0] + residual.shape[0]
    shape = pltpu.VMEM((1, rows * 3 // 2, LANES), jnp.bfloat16)
    args = [pltpu.with_memory_space_constraint(a, pltpu.HBM) for a in (points, direction, residual)]
    return pl.pallas_call(
        pack_kernel,
        out_shape=shape,
        in_specs=[pl.BlockSpec(memory_space=pltpu.HBM)] * 3,
        out_specs=in_vmem(),
        scratch_shapes=[pltpu.VMEM(a.shape, a.dtype) for a in args] + [pltpu.SemaphoreType.DMA((3,))],
        compiler_params=pltpu.CompilerParams(vmem_limit_bytes=VMEM_BYTES),
    )(*args)


def unpack(packs, dim, probes):
    columns = 3 * LANES
    outs = (
        jax.ShapeDtypeStruct((1, dim + probes, columns), packs.dtype),
        jax.ShapeDtypeStruct((probes, columns), jnp.float32),
    )
    return call(unpack_kernel, outs, (packs,))


def add_fold(own, piece, before, dim):
    if piece.shape[0] == 2:
        full = jax.ShapeDtypeStruct(before.shape, before.dtype)
        return call(functools.partial(fold_kernel, dim), full, (own, piece, before), 1)
    whole = lambda index: (0, 0)
    return pl.pallas_call(
        functools.partial(long_fold_kernel, dim),
        grid=(piece.shape[0] // 2,),
        out_shape=jax.ShapeDtypeStruct(before.shape, before.dtype),
        in_specs=[
            pl.BlockSpec(own.shape, lambda index: (0, 0, 0)),
            pl.BlockSpec((2, *piece.shape[1:]), lambda index: (index, 0, 0)),
            pl.BlockSpec(before.shape, whole),
        ],
        out_specs=pl.BlockSpec(before.shape, whole),
        compiler_params=pltpu.CompilerParams(vmem_limit_bytes=VMEM_BYTES),
    )(own, piece, before)


def strides(count):
    found = []
    while count > 1:
        assert count % 2 == 0
        count //= 2
        found.append(count)
    return found


def swapped(array, count, stride):
    return lax.ppermute(array, AXES, [(i, i ^ stride) for i in range(count)])


def make_body(count):
    far, near, middle, *others, cores = strides(count)

    def body(points, direction, residual, solution):
        dim, width = points.shape
        probes = direction.shape[0]
        full = jax.ShapeDtypeStruct((probes, 4 * width), jnp.float32)
        table = jax.ShapeDtypeStruct((8, probes), jnp.float32)
        packed = pack(points, direction, residual)
        pair = jnp.concatenate([packed, swapped(packed, count, far)], axis=0)
        other = swapped(pair, count, middle)
        half, rest = unpack(pair, dim, probes)
        other_half, other_rest = unpack(other, dim, probes)
        own = jnp.concatenate([half, other_half], axis=0)
        other_beside = swapped(half, count, near | middle)
        beside = swapped(half, count, near)
        crossed = swapped(own, count, cores)
        applied = call(functools.partial(first_fold_kernel, dim), full, (own,), 1)
        beside = call(
            join_kernel,
            jax.ShapeDtypeStruct(own.shape, own.dtype),
            (other_beside, beside, applied),
        )
        applied = add_fold(own, crossed, applied, dim)
        blocks = [own, beside]
        for stride in others:
            blocks.append(swapped(jnp.concatenate(blocks, axis=0), count, stride))
        for block in blocks[1:]:
            crossed = swapped(block, count, cores)
            applied = add_fold(own, block, applied, dim)
            if block is not blocks[-1]:
                applied = add_fold(own, crossed, applied, dim)
        if crossed.shape[0] == 2:
            applied, sums = call(
                functools.partial(last_kernel, dim),
                (full, table),
                (own, crossed, applied, rest, other_rest),
                1,
            )
        else:
            applied = add_fold(own, crossed, applied, dim)
            sums = call(
                functools.partial(sums_kernel, dim), table, (own, rest, other_rest, applied)
            )
        for stride in others:
            sums = sums + swapped(sums, count, stride)
        sums = (
            sums
            + swapped(sums, count, near)
            + swapped(sums, count, near | cores)
            + swapped(sums, count, cores)
        )
        start = 2 * LANES
        applied = jnp.concatenate([applied[:, :LANES], applied[:, start : start + width - LANES]], axis=1)
        image = applied + noise_level * direction
        old_norm, curvature, cross, image_norm = sums[0], sums[1], sums[2], sums[3]
        step_size = old_norm / curvature
        solution_next = solution + step_size[:, None] * direction
        residual_next = residual - step_size[:, None] * image
        new_norm = old_norm + step_size * (step_size * image_norm - 2.0 * cross)
        direction_next = residual_next + (new_norm / (old_norm + 1e-06))[:, None] * direction
        return (solution_next, residual_next, direction_next)

    return body


def solution(mesh):
    placed = P(None, ("groups", "row", "col"))
    return jax.shard_map(
        make_body(mesh.shape["row"] * mesh.shape["col"]),
        mesh=mesh,
        in_specs=(placed,) * 4,
        out_specs=(placed,) * 3,
        check_vma=False,
    )
```

```python
import functools
import math

import jax
import jax.numpy as jnp
from jax import lax
from jax.experimental import pallas as pl
from jax.experimental.pallas import tpu as pltpu
from jax.sharding import PartitionSpec as P

amplitude = 1.0
length_square = 32.0
noise_level = 0.5

AXES = ("row", "col")
LANES = 128
VMEM_BYTES = 32 << 20
RATE = math.log2(math.e) / length_square
SHIFT = math.log2(amplitude)


def in_vmem():
    return pl.BlockSpec(memory_space=pltpu.VMEM)


def pack_kernel(
    points_hbm, direction_hbm, residual_hbm, packed_ref, points_ref, direction_ref, residual_ref, arrived
):
    copies = [
        pltpu.make_async_copy(source, target, arrived.at[index])
        for index, (source, target) in enumerate(
            (
                (points_hbm, points_ref),
                (direction_hbm, direction_ref),
                (residual_hbm, residual_ref),
            )
        )
    ]
    for copy in copies:
        copy.start()
    for copy in copies:
        copy.wait()
    fields = jnp.concatenate(
        [
            points_ref[...],
            direction_ref[...].astype(jnp.bfloat16),
            residual_ref[...].astype(jnp.bfloat16),
        ],
        axis=0,
    )
    height = fields.shape[0]
    packed_ref[0, :height] = fields[:, :LANES]
    packed_ref[0, height:] = jnp.concatenate(
        [fields[: height // 2, LANES:], fields[height // 2 :, LANES:]], axis=1
    )


def unpack_kernel(packs_ref, held_ref, residual_ref):
    height = packs_ref.shape[1] * 2 // 3
    side = LANES // 2
    first, second = packs_ref[0, height:], packs_ref[1, height:]
    tails = jnp.concatenate(
        [
            jnp.concatenate([first[:, :side], second[:, :side]], axis=1),
            jnp.concatenate([first[:, side:], second[:, side:]], axis=1),
        ],
        axis=0,
    )
    rows = held_ref.shape[1]
    for index, part in enumerate((packs_ref[0, :height], packs_ref[1, :height], tails)):
        span = slice(index * LANES, (index + 1) * LANES)
        held_ref[0, :, span] = part[:rows]
        residual_ref[:, span] = part[rows:].astype(jnp.float32)


def read(ref):
    return jnp.concatenate([ref[index] for index in range(ref.shape[0])], axis=1)


def widened(points, own):
    values = points.astype(jnp.float32)
    half = -0.5 * jnp.sum(values * values, axis=0, keepdims=True)
    high = half.astype(jnp.bfloat16).astype(jnp.float32)
    middle = (half - high).astype(jnp.bfloat16).astype(jnp.float32)
    low = half - high - middle
    row = lax.broadcasted_iota(jnp.int32, (16, points.shape[1]), 0)
    base = 0 if own else 3
    extra = jnp.where(row < 6, 1.0, 0.0)
    extra = jnp.where(row == base, high, extra)
    extra = jnp.where(row == base + 1, middle, extra)
    extra = jnp.where(row == base + 2, low, extra)
    return jnp.concatenate([points, extra.astype(jnp.bfloat16)], axis=0)


def fold(own, piece, applied, dim):
    half = lax.dot_general(
        widened(piece[:dim], False),
        widened(own[:dim], True),
        (((0,), (0,)), ((), ())),
        preferred_element_type=jnp.float32,
    )
    kernel = jnp.exp2(half * RATE + SHIFT).astype(jnp.bfloat16)
    part = lax.dot_general(
        piece[dim:], kernel, (((1,), (0,)), ((), ())), preferred_element_type=jnp.float32
    )
    return part if applied is None else applied + part


def first_fold_kernel(dim, own_ref, applied_ref):
    own = read(own_ref)
    applied_ref[...] = fold(own, own, None, dim)


def fold_kernel(dim, own_ref, piece_ref, before_ref, applied_ref):
    applied_ref[...] = fold(read(own_ref), read(piece_ref), before_ref[...], dim)


def two_folds_kernel(dim, own_ref, first_ref, second_ref, before_ref, applied_ref):
    own = read(own_ref)
    applied = fold(own, read(first_ref), before_ref[...], dim)
    applied_ref[...] = fold(own, read(second_ref), applied, dim)


def join_kernel(first_ref, second_ref, after_ref, joined_ref):
    del after_ref
    count = first_ref.shape[0]
    joined_ref[:count] = first_ref[...]
    joined_ref[count:] = second_ref[...]


def long_fold_kernel(dim, own_ref, piece_ref, before_ref, applied_ref):
    @pl.when(pl.program_id(0) == 0)
    def _():
        applied_ref[...] = before_ref[...]

    applied_ref[...] = fold(read(own_ref), read(piece_ref), applied_ref[...], dim)


def sums_kernel(dim, own_ref, residual_ref, other_residual_ref, applied_ref, sums_ref):
    residual = jnp.concatenate([residual_ref[...], other_residual_ref[...]], axis=1)
    direction = read(own_ref)[dim:].astype(jnp.float32)
    image = applied_ref[...] + noise_level * direction
    lane = lax.broadcasted_iota(jnp.int32, (image.shape[0], LANES), 1)
    table = jnp.zeros((image.shape[0], LANES), jnp.float32)
    products = (residual * residual, direction * image, residual * image, image * image)
    for index, product in enumerate(products):
        table = jnp.where(lane == index, jnp.sum(product, axis=1, keepdims=True), table)
    sums_ref[...] = table.T[:8]


def last_kernel(dim, own_ref, piece_ref, before_ref, residual_ref, other_residual_ref, applied_ref, sums_ref):
    fold_kernel(dim, own_ref, piece_ref, before_ref, applied_ref)
    sums_kernel(dim, own_ref, residual_ref, other_residual_ref, applied_ref, sums_ref)


def call(kernel, outs, args, folds=0):
    columns, dim, probes = 768, 80, 32
    cost = None
    if folds:
        count = folds * columns * columns
        cost = pl.CostEstimate(
            flops=2 * count * (dim + probes), bytes_accessed=count, transcendentals=count
        )
    return pl.pallas_call(
        kernel,
        out_shape=outs,
        in_specs=[in_vmem()] * len(args),
        out_specs=jax.tree.map(lambda _: in_vmem(), outs),
        compiler_params=pltpu.CompilerParams(vmem_limit_bytes=VMEM_BYTES),
        cost_estimate=cost,
    )(*args)


def pack(points, direction, residual):
    rows = points.shape[0] + direction.shape[0] + residual.shape[0]
    shape = pltpu.VMEM((1, rows * 3 // 2, LANES), jnp.bfloat16)
    args = [pltpu.with_memory_space_constraint(a, pltpu.HBM) for a in (points, direction, residual)]
    return pl.pallas_call(
        pack_kernel,
        out_shape=shape,
        in_specs=[pl.BlockSpec(memory_space=pltpu.HBM)] * 3,
        out_specs=in_vmem(),
        scratch_shapes=[pltpu.VMEM(a.shape, a.dtype) for a in args] + [pltpu.SemaphoreType.DMA((3,))],
        compiler_params=pltpu.CompilerParams(vmem_limit_bytes=VMEM_BYTES),
    )(*args)


def unpack(packs, dim, probes):
    columns = 3 * LANES
    outs = (
        jax.ShapeDtypeStruct((1, dim + probes, columns), packs.dtype),
        jax.ShapeDtypeStruct((probes, columns), jnp.float32),
    )
    return call(unpack_kernel, outs, (packs,))


def add_fold(own, piece, before, dim):
    if piece.shape[0] == 2:
        full = jax.ShapeDtypeStruct(before.shape, before.dtype)
        return call(functools.partial(fold_kernel, dim), full, (own, piece, before), 1)
    whole = lambda index: (0, 0)
    return pl.pallas_call(
        functools.partial(long_fold_kernel, dim),
        grid=(piece.shape[0] // 2,),
        out_shape=jax.ShapeDtypeStruct(before.shape, before.dtype),
        in_specs=[
            pl.BlockSpec(own.shape, lambda index: (0, 0, 0)),
            pl.BlockSpec((2, *piece.shape[1:]), lambda index: (index, 0, 0)),
            pl.BlockSpec(before.shape, whole),
        ],
        out_specs=pl.BlockSpec(before.shape, whole),
        compiler_params=pltpu.CompilerParams(vmem_limit_bytes=VMEM_BYTES),
    )(own, piece, before)


def strides(count):
    found = []
    while count > 1:
        assert count % 2 == 0
        count //= 2
        found.append(count)
    return found


def swapped(array, count, stride):
    return lax.ppermute(array, AXES, [(i, i ^ stride) for i in range(count)])


def make_body(count):
    far, near, middle, *others, cores = strides(count)

    def body(points, direction, residual, solution):
        dim, width = points.shape
        probes = direction.shape[0]
        full = jax.ShapeDtypeStruct((probes, 4 * width), jnp.float32)
        table = jax.ShapeDtypeStruct((8, probes), jnp.float32)
        packed = pack(points, direction, residual)
        pair = jnp.concatenate([packed, swapped(packed, count, far)], axis=0)
        other = swapped(pair, count, middle)
        half, rest = unpack(pair, dim, probes)
        other_half, other_rest = unpack(other, dim, probes)
        own = jnp.concatenate([half, other_half], axis=0)
        other_beside = swapped(half, count, near | middle)
        beside = swapped(half, count, near)
        crossed = swapped(own, count, cores)
        applied = call(functools.partial(first_fold_kernel, dim), full, (own,), 1)
        beside = call(
            join_kernel,
            jax.ShapeDtypeStruct(own.shape, own.dtype),
            (other_beside, beside, applied),
        )
        applied = call(
            functools.partial(two_folds_kernel, dim), full, (own, crossed, beside, applied), 2
        )
        blocks = [own, beside]
        for stride in others:
            blocks.append(swapped(jnp.concatenate(blocks, axis=0), count, stride))
        for block in blocks[1:]:
            crossed = swapped(block, count, cores)
            if block is not beside:
                applied = add_fold(own, block, applied, dim)
            if block is not blocks[-1]:
                applied = add_fold(own, crossed, applied, dim)
        if crossed.shape[0] == 2:
            applied, sums = call(
                functools.partial(last_kernel, dim),
                (full, table),
                (own, crossed, applied, rest, other_rest),
                1,
            )
        else:
            applied = add_fold(own, crossed, applied, dim)
            sums = call(
                functools.partial(sums_kernel, dim), table, (own, rest, other_rest, applied)
            )
        for stride in others:
            sums = sums + swapped(sums, count, stride)
        sums = (
            sums
            + swapped(sums, count, near)
            + swapped(sums, count, near | cores)
            + swapped(sums, count, cores)
        )
        start = 2 * LANES
        applied = jnp.concatenate([applied[:, :LANES], applied[:, start : start + width - LANES]], axis=1)
        image = applied + noise_level * direction
        old_norm, curvature, cross, image_norm = sums[0], sums[1], sums[2], sums[3]
        step_size = old_norm / curvature
        solution_next = solution + step_size[:, None] * direction
        residual_next = residual - step_size[:, None] * image
        new_norm = old_norm + step_size * (step_size * image_norm - 2.0 * cross)
        direction_next = residual_next + (new_norm / (old_norm + 1e-06))[:, None] * direction
        return (solution_next, residual_next, direction_next)

    return body


def solution(mesh):
    placed = P(None, ("groups", "row", "col"))
    return jax.shard_map(
        make_body(mesh.shape["row"] * mesh.shape["col"]),
        mesh=mesh,
        in_specs=(placed,) * 4,
        out_specs=(placed,) * 3,
        check_vma=False,
    )
```
